256 devices in a mesh: mom: 16 (over z_hi, y, core), hist: 16 (over z_lo, x).
Axes of the slice: x: 4, y: 4, z: 8 (z_hi: 2, z_lo: 4; z = z_hi * 4 + z_lo), core: 2. Of those that a mesh axis runs over, the one named last changes fastest.
Arguments:
- green_row: float32 [6144, 256, 128], P('hist', 'mom'), may hold values from -6 to 6
- green_col: float32 [6144, 256, 128], P('hist', 'mom'), may hold values from -6 to 6
- screen: float32 [6144, 256, 128], P(('hist', 'mom')), may hold values from -2.5 to 2.5
- filled: int32 [16], P('hist'), may hold values from 1 to 384, 4608 in all
- sigma_mix: float32 [400, 256, 128], P('hist', 'mom'), may hold values from -6 to 6
- green_mix: float32 [400, 256, 128], P('hist', 'mom'), may hold values from -6 to 6
- green_now: float32 [256, 128], P('mom'), may hold values from -6 to 6
- hamilton: float32 [256, 128], P('mom'), may hold values from -2 to 2
Outputs:
- collision: float32 [256, 128], P('mom')
- green_next: float32 [256, 128], P('mom')
The draws below stay inside these ranges and needn't reach their ends.
Inputs may be any that keep to these rules, and one draw needn't show every extreme that they name: filled[h] counts the used past-time slots of history group h, which are its first ones; the counts sum to 4608.
All inputs are finite; a program needn't handle non-finite values.
Results may differ from the reference program's by a relative error of at most 0.0003.
Values sent between devices are 32-bit elements; how exact they have to be, the bound alone decides.
No kernel may reach another device: no remote copies, remote signals or barrier semaphores. Data moves between devices by JAX's collectives and lax.ppermute only.
A program may use at most 128 MiB of HBM per device.

```python
import math
import jax
import jax.numpy as jnp
import numpy as np
from jax import lax

LAT = 16
K = 256
ORBITAL_COUNT = 8
NTAU = 400
TB = 384
TPAST = 6144
USED = 4608
N_HIST = 16


def shard_levels(key, shape, cuts, least, high):
    gain = 1.0
    for axis_at, shards_of in cuts:
        steps = jax.random.uniform(jax.random.fold_in(jax.random.fold_in(key, 6), axis_at), (shards_of,), jnp.float32, least / len(cuts), high / len(cuts))
        gain = gain * jnp.repeat(jnp.exp(steps), shape[axis_at] // shards_of).reshape((-1,) + (1,) * (len(shape) - 1 - axis_at))
    return gain


def length_profile(amount, total, most, skew):
    loads = [(1 << 20) // math.isqrt(grade ** skew) + 1 for grade in range(2, amount + 1)]
    surplus, holding = total - most - (amount - 1), [1] * (amount - 1)
    while surplus > 0:
        movable = [i for i in range(amount - 1) if holding[i] < most]
        pool, remaining = sum([loads[i] for i in movable]), surplus
        for i in movable:
            extra = min(most - holding[i], max(1, remaining * loads[i] // pool), surplus)
            holding[i] = holding[i] + extra
            surplus = surplus - extra
    return np.array([most] + holding)


def ragged_sizes(rng, number_of, total, limit, skew):
    if number_of == 2:
        one = jax.random.randint(rng, (), max(1, total - limit), min(limit, total - 1) + 1)
        return jnp.stack([one, total - one])
    lengths = jnp.asarray(length_profile(number_of, total, limit, skew), jnp.int32)
    pairs = (number_of - 1) // 2
    source_of, receiver = lengths[1:1 + 2 * pairs:2], lengths[2:2 + 2 * pairs:2]
    margin = jnp.minimum(source_of - 1, limit - receiver)
    shifted = jax.random.randint(jax.random.fold_in(rng, 1), (pairs,), 0, 1 << 20) % (margin + 1)
    lengths = lengths.at[1:1 + 2 * pairs:2].set(source_of - shifted).at[2:2 + 2 * pairs:2].set(receiver + shifted)
    return lengths[jax.random.permutation(jax.random.fold_in(rng, 2), number_of)]


def gaussian(own_key, shape, scale, reach, split=(), held_as=jnp.bfloat16):
    array = jax.random.normal(own_key, shape, jnp.float32) * scale
    if len(split) > 0:
        array = shard_levels(own_key, shape, split, -0.22, 0.18) * array
    return jnp.clip(array, min=-reach, max=reach).astype(held_as)


def setup_inputs(seed: int = 0) -> dict:
    streams_of = jax.random.split(jax.random.key(seed), 9)
    return {
        "green_row": gaussian(streams_of[0], (TPAST, K, 2 * ORBITAL_COUNT * ORBITAL_COUNT), 1.0, 6.0, ((0, 16), (1, 16)), jnp.float32),
        "green_col": gaussian(streams_of[1], (TPAST, K, 2 * ORBITAL_COUNT * ORBITAL_COUNT), 1.0, 6.0, ((0, 16), (1, 16)), jnp.float32),
        "screen": gaussian(streams_of[2], (TPAST, K, 2 * ORBITAL_COUNT * ORBITAL_COUNT), 0.35, 2.5, ((0, 256),), jnp.float32),
        "filled": ragged_sizes(streams_of[3], N_HIST, USED, TB, 2).astype(jnp.int32),
        "sigma_mix": gaussian(streams_of[4], (NTAU, K, 2 * ORBITAL_COUNT * ORBITAL_COUNT), 1.0, 6.0, ((0, 16), (1, 16)), jnp.float32),
        "green_mix": gaussian(streams_of[5], (NTAU, K, 2 * ORBITAL_COUNT * ORBITAL_COUNT), 1.0, 6.0, ((0, 16), (1, 16)), jnp.float32),
        "green_now": gaussian(streams_of[6], (K, 2 * ORBITAL_COUNT * ORBITAL_COUNT), 1.0, 6.0, ((0, 16),), jnp.float32),
        "hamilton": gaussian(streams_of[7], (K, 2 * ORBITAL_COUNT * ORBITAL_COUNT), ORBITAL_COUNT ** -0.5, 2.0, ((0, 16),), jnp.float32),
    }


MEMORY_WEIGHT = 0.01
MIX_WEIGHT = 0.01
TIME_STEP = 0.1
HIGHEST = lax.Precision.HIGHEST


def axis_tables():
    points = jnp.arange(LAT, dtype=jnp.int32)
    phases = (points[:, None] * points[None, :]) % LAT
    angles = phases.astype(jnp.float32) * (2.0 * jnp.pi / LAT)
    return jnp.cos(angles), jnp.sin(angles)


def turn_axis(re_part, im_part, cosine, sine_table, orient, form):
    cos_re = jnp.einsum(form, cosine, re_part, precision=HIGHEST)
    cos_im = jnp.einsum(form, cosine, im_part, precision=HIGHEST)
    sin_re = jnp.einsum(form, sine_table, re_part, precision=HIGHEST)
    sin_im = jnp.einsum(form, sine_table, im_part, precision=HIGHEST)
    return cos_re - orient * sin_im, cos_im + orient * sin_re


def matrix_sum(left_rows, right_rows, weights):
    slot_count, points, row_width = left_rows.shape
    left_blocks = left_rows.reshape(slot_count, points, 2, ORBITAL_COUNT, ORBITAL_COUNT)
    right_blocks = right_rows.reshape(slot_count, points, 2, ORBITAL_COUNT, ORBITAL_COUNT) * weights[:, None, None, None, None]

    def contract(first, second):
        return jnp.einsum("skab,skbc->kac", first, second, precision=HIGHEST)

    real_sum = contract(left_blocks[:, :, 0], right_blocks[:, :, 0]) - contract(left_blocks[:, :, 1], right_blocks[:, :, 1])
    imag_sum = contract(left_blocks[:, :, 0], right_blocks[:, :, 1]) + contract(left_blocks[:, :, 1], right_blocks[:, :, 0])
    return jnp.concatenate([real_sum.reshape(points, ORBITAL_COUNT * ORBITAL_COUNT), imag_sum.reshape(points, ORBITAL_COUNT * ORBITAL_COUNT)], axis=-1)


def group_history(green_rows, green_cols, screen_rows, used_slots, cosine, sine_table):
    slot_count = green_rows.shape[0]
    halfway = ORBITAL_COUNT * ORBITAL_COUNT
    lattice_grid = green_rows.reshape(slot_count, LAT, LAT, 2 * halfway)
    re_part = lattice_grid[..., :halfway]
    im_part = lattice_grid[..., halfway:]
    re_part, im_part = turn_axis(re_part, im_part, cosine, sine_table, 1.0, "kr,skyc->sryc")
    re_part, im_part = turn_axis(re_part, im_part, cosine, sine_table, 1.0, "kr,sxkc->sxrc")
    re_part = re_part / K
    im_part = im_part / K
    screen_grid = screen_rows.reshape(slot_count, LAT, LAT, 2 * halfway)
    screen_re = screen_grid[..., :halfway]
    screen_im = screen_grid[..., halfway:]
    prod_re = re_part * screen_re - im_part * screen_im
    prod_im = re_part * screen_im + im_part * screen_re
    sig_re, sig_im = turn_axis(-prod_im, prod_re, cosine, sine_table, -1.0, "kr,skyc->sryc")
    sig_re, sig_im = turn_axis(sig_re, sig_im, cosine, sine_table, -1.0, "kr,sxkc->sxrc")
    sigma = jnp.concatenate([sig_re, sig_im], axis=-1).reshape(slot_count, K, 2 * halfway)
    valid = (jnp.arange(slot_count, dtype=jnp.int32) < used_slots).astype(jnp.float32)
    return matrix_sum(sigma, green_cols, valid)


def complex_product(left_blocks, right_blocks):
    def contract(first, second):
        return jnp.einsum("kab,kbc->kac", first, second, precision=HIGHEST)

    real_part = contract(left_blocks[:, 0], right_blocks[:, 0]) - contract(left_blocks[:, 1], right_blocks[:, 1])
    imag_part = contract(left_blocks[:, 0], right_blocks[:, 1]) + contract(left_blocks[:, 1], right_blocks[:, 0])
    return real_part, imag_part


def advance(collision, green_now, hamilton):
    resident_rows, row_width = green_now.shape
    green_blocks = green_now.reshape(resident_rows, 2, ORBITAL_COUNT, ORBITAL_COUNT)
    ham_blocks = hamilton.reshape(resident_rows, 2, ORBITAL_COUNT, ORBITAL_COUNT)
    collision_tiles = collision.reshape(resident_rows, 2, ORBITAL_COUNT, ORBITAL_COUNT)
    left_re, left_im = complex_product(ham_blocks, green_blocks)
    right_re, right_im = complex_product(green_blocks, ham_blocks)
    comm_re = left_re - right_re
    comm_im = left_im - right_im
    hermitian_real = collision_tiles[:, 0] + jnp.swapaxes(collision_tiles[:, 0], 1, 2)
    hermitian_imaginary = collision_tiles[:, 1] - jnp.swapaxes(collision_tiles[:, 1], 1, 2)
    next_re = green_blocks[:, 0] + TIME_STEP * comm_im - TIME_STEP * hermitian_real
    next_im = green_blocks[:, 1] - TIME_STEP * comm_re - TIME_STEP * hermitian_imaginary
    return jnp.stack([next_re, next_im], axis=1).reshape(resident_rows, row_width)


def reference(green_row, green_col, screen, filled, sigma_mix, green_mix, green_now, hamilton):
    cosine, sine_table = axis_tables()
    groups = filled.shape[0]
    row_width = green_row.shape[-1]
    stacked = (green_row.reshape(groups, TB, K, row_width), green_col.reshape(groups, TB, K, row_width),
               screen.reshape(groups, TB, K, row_width), filled)

    def one_group(pieces):
        return group_history(pieces[0], pieces[1], pieces[2], pieces[3], cosine, sine_table)

    history = jnp.sum(lax.map(one_group, stacked), axis=0)
    summed = matrix_sum(sigma_mix, green_mix, jnp.ones((sigma_mix.shape[0],), jnp.float32))
    mixed_contribution = jnp.concatenate([summed[:, ORBITAL_COUNT * ORBITAL_COUNT:], -summed[:, :ORBITAL_COUNT * ORBITAL_COUNT]], axis=-1)
    collision = MEMORY_WEIGHT * history + MIX_WEIGHT * mixed_contribution
    return collision, advance(collision, green_now, hamilton)
```

```python
import functools
import math

import jax
import jax.numpy as jnp
import numpy as np
from jax import lax
from jax.experimental import pallas as pl
from jax.experimental.pallas import tpu as pltpu
from jax.sharding import PartitionSpec as P

LAT = 16
ORBITAL_COUNT = 8
HALF = ORBITAL_COUNT * ORBITAL_COUNT
ROW = 2 * HALF
MEMORY_WEIGHT = 0.01
MIX_WEIGHT = 0.01
TIME_STEP = 0.1
HIGHEST = lax.Precision.HIGHEST
VMEM_LIMIT = 40 * 1024 * 1024


def split(values):
    high = values.astype(jnp.bfloat16)
    return high, (values - high.astype(jnp.float32)).astype(jnp.bfloat16)


def lattice_tables():
    points = np.arange(LAT)
    kx, ky = np.repeat(points, LAT), np.tile(points, LAT)
    phase = (kx[:, None] * kx[None, :] + ky[:, None] * ky[None, :]) % LAT
    angle = phase * (2.0 * math.pi / LAT)
    table = np.concatenate([np.cos(angle), np.sin(angle)]).astype(np.float32)
    high = table.astype(jnp.bfloat16)
    return high, (table - high.astype(np.float32)).astype(jnp.bfloat16)


def dot(first, second):
    return lax.dot_general(first, second, (((1,), (0,)), ((), ())), preferred_element_type=jnp.float32)


def times_i(values, low):
    turned = pltpu.roll(values, HALF, 1)
    return jnp.where(low, -turned, turned)


def sigma_kernel(high_ref, low_ref, green_ref, screen_ref, out_ref):
    points = LAT * LAT
    slots = screen_ref.shape[0]
    lane = lax.broadcasted_iota(jnp.int32, (points, ROW), 1)
    first = lane < HALF

    def turn(pair, sign):
        parts = [split(p) for p in pair]
        high = jnp.concatenate([p[0] for p in parts], axis=1)
        low = jnp.concatenate([p[1] for p in parts], axis=1)
        both = dot(high_ref[...], high) + (dot(high_ref[...], low) + dot(low_ref[...], high))
        out = []
        for i in range(len(pair)):
            here = both[:, i * ROW : (i + 1) * ROW]
            out.append(here[:points] + sign * times_i(here[points:], first))
        return out

    for s in range(0, slots, 2):
        space = turn([green_ref[:, s + i].reshape(points, ROW) for i in range(2)], 1.0)
        product = []
        for i in range(2):
            w = screen_ref[s + i] * (1.0 / points)
            w_turned = pltpu.roll(w, HALF, 1)
            g = space[i]
            g_turned = pltpu.roll(g, HALF, 1)
            product.append(g_turned * jnp.where(first, -w, w_turned) - g * jnp.where(first, w_turned, w))
        sigma = turn(product, -1.0)
        for i in range(2):
            out_ref[:, :, s + i, :] = sigma[i].reshape(LAT, LAT, ROW)


def sigma_of(green, screen):
    slots = screen.shape[0]
    step = 8
    high, low = lattice_tables()
    points = LAT * LAT
    return pl.pallas_call(
        sigma_kernel,
        grid=(slots // step,),
        in_specs=[
            pl.BlockSpec((2 * points, points), lambda i: (0, 0)),
            pl.BlockSpec((2 * points, points), lambda i: (0, 0)),
            pl.BlockSpec((LAT, step, LAT, ROW), lambda i: (0, i, 0, 0)),
            pl.BlockSpec((step, points, ROW), lambda i: (i, 0, 0)),
        ],
        out_specs=pl.BlockSpec((LAT, LAT, step, ROW), lambda i: (0, 0, i, 0)),
        out_shape=jax.ShapeDtypeStruct((LAT, LAT, slots, ROW), jnp.float32),
        compiler_params=pltpu.CompilerParams(vmem_limit_bytes=VMEM_LIMIT),
        cost_estimate=pl.CostEstimate(flops=slots * 12 * points * points * ROW, bytes_accessed=3 * slots * points * ROW * 4, transcendentals=0),
        name="sigma",
    )(jnp.asarray(high), jnp.asarray(low), green, screen)


def history_kernel(high_ref, low_ref, sigma_ref, spread_ref, mixed_ref, out_ref):
    owners, _, slots, _ = sigma_ref.shape
    lane = lax.broadcasted_iota(jnp.int32, (ORBITAL_COUNT, ROW), 1)
    sub = lax.broadcasted_iota(jnp.int32, (ORBITAL_COUNT, ROW), 0)
    inner = lane % ORBITAL_COUNT
    blocks = []
    for k in range(LAT):
        rows = sigma_ref[:, k].reshape(owners * slots, ROW)
        s_high, s_low = split(rows)
        c_high, c_low = high_ref[k], low_ref[k]
        outer = dot(c_high, s_high) + (dot(c_high, s_low) + dot(c_low, s_high))
        outer = outer.reshape(2, ORBITAL_COUNT, ORBITAL_COUNT, ROW)
        for part in range(2):
            picked = jnp.zeros((ORBITAL_COUNT, ROW), jnp.float32)
            for b in range(ORBITAL_COUNT):
                picked = jnp.where(inner == b, outer[part, b], picked)
            blocks.append(picked)
    picked = jnp.concatenate(blocks, axis=0)
    p_high, p_rest = split(picked)
    p_low = p_rest
    spread = spread_ref[...]
    summed = dot(p_high, spread) + dot(p_low, spread)
    summed = summed.reshape(2 * LAT, ORBITAL_COUNT, ROW)
    summed = jnp.sum(jnp.where((inner == sub)[None], summed, 0.0), axis=1).reshape(LAT, 2, ROW)
    low_half = lax.broadcasted_iota(jnp.int32, (LAT, ROW), 1) < HALF
    out_ref[...] = MEMORY_WEIGHT * (summed[:, 0] + times_i(summed[:, 1], low_half)) + mixed_ref[...]


def spread_table():
    group = np.arange(ROW) // ORBITAL_COUNT
    return (group[:, None] == group[None, :]).astype(jnp.bfloat16)


def history_of(high, low, sigma, mixed):
    return pl.pallas_call(
        history_kernel,
        out_shape=jax.ShapeDtypeStruct((LAT, ROW), jnp.float32),
        compiler_params=pltpu.CompilerParams(vmem_limit_bytes=VMEM_LIMIT),
        cost_estimate=pl.CostEstimate(flops=16 * 6 * 384 * ROW * ROW, bytes_accessed=2 * 384 * 16 * ROW * 4, transcendentals=0),
        name="history",
    )(high, low, sigma, jnp.asarray(spread_table()), mixed)


def complex_product(left, right):
    def contract(first, second):
        return jnp.einsum("kab,kbc->kac", first, second, precision=HIGHEST)

    return (
        contract(left[:, 0], right[:, 0]) - contract(left[:, 1], right[:, 1]),
        contract(left[:, 0], right[:, 1]) + contract(left[:, 1], right[:, 0]),
    )


def free_step(green_now, hamilton):
    shape = (green_now.shape[0], 2, ORBITAL_COUNT, ORBITAL_COUNT)
    green, ham = green_now.reshape(shape), hamilton.reshape(shape)
    left_re, left_im = complex_product(ham, green)
    right_re, right_im = complex_product(green, ham)
    moved = jnp.stack([left_im - right_im, right_re - left_re], axis=1)
    return green_now + TIME_STEP * moved.reshape(green_now.shape)


def mixed_sum(sigma_mix, green_mix):
    taus, points, _ = sigma_mix.shape
    left = sigma_mix.reshape(taus, points, 2, ORBITAL_COUNT, ORBITAL_COUNT)
    right = green_mix.reshape(taus, points, 2, ORBITAL_COUNT, ORBITAL_COUNT)

    def contract(first, second):
        return jnp.einsum("skab,skbc->kac", first, second, precision=HIGHEST).reshape(points, HALF)

    real = contract(left[:, :, 0], right[:, :, 0]) - contract(left[:, :, 1], right[:, :, 1])
    imag = contract(left[:, :, 0], right[:, :, 1]) + contract(left[:, :, 1], right[:, :, 0])
    return MIX_WEIGHT * jnp.concatenate([imag, -real], axis=-1)


def finish_kernel(parts_ref, free_ref, adjoint_ref, collision_ref, next_ref):
    collision = parts_ref[0]
    for i in range(1, parts_ref.shape[0]):
        collision = collision + parts_ref[i]
    high, rest = split(collision)
    middle, low = split(collision - high.astype(jnp.float32))
    adjoint = adjoint_ref[...]
    turned = dot(high, adjoint) + (dot(middle, adjoint) + dot(low, adjoint))
    collision_ref[...] = collision
    next_ref[...] = free_ref[...] - TIME_STEP * (collision + turned)


def adjoint_table():
    table = np.zeros((ROW, ROW), np.float32)
    for a in range(ORBITAL_COUNT):
        for c in range(ORBITAL_COUNT):
            table[a * ORBITAL_COUNT + c, c * ORBITAL_COUNT + a] = 1.0
            table[HALF + a * ORBITAL_COUNT + c, HALF + c * ORBITAL_COUNT + a] = -1.0
    return table.astype(jnp.bfloat16)


def finish(parts, free):
    out = jax.ShapeDtypeStruct(free.shape, jnp.float32)
    return pl.pallas_call(finish_kernel, out_shape=(out, out), name="finish")(parts, free, jnp.asarray(adjoint_table()))


def per_device(green_row, green_col, screen, filled, sigma_mix, green_mix, green_now, hamilton):
    slot_count, local_k, _ = green_row.shape
    owners = lax.axis_size("mom")
    own = slot_count // owners
    moved = lax.all_to_all(green_row.reshape(owners, own, local_k, ROW), "mom", 0, 0)
    sigma = sigma_of(moved, screen)
    arrived = lax.all_to_all(sigma, "mom", 0, 0)

    valid = jnp.arange(slot_count, dtype=jnp.int32) < filled[0]
    column = jnp.where(valid[:, None, None], green_col, 0.0)
    column = jnp.transpose(column, (1, 2, 0))
    high = lax.reduce_precision(column, 8, 7)
    high, low = high.astype(jnp.bfloat16), (column - high).astype(jnp.bfloat16)
    partial_sum = history_of(high, low, arrived, mixed_sum(sigma_mix, green_mix))
    groups = lax.axis_size("hist")
    parts = lax.all_to_all(jnp.broadcast_to(partial_sum[None], (groups, local_k, ROW)), "hist", 0, 0)
    return finish(parts, free_step(green_now, hamilton))


def solution(mesh):
    return jax.shard_map(
        per_device,
        mesh=mesh,
        in_specs=(
            P("hist", "mom", None),
            P("hist", "mom", None),
            P(("hist", "mom"), None, None),
            P("hist"),
            P("hist", "mom", None),
            P("hist", "mom", None),
            P("mom", None),
            P("mom", None),
        ),
        out_specs=(P("mom", None), P("mom", None)),
        check_vma=False,
    )
```

```python
import functools
import math

import jax
import jax.numpy as jnp
import numpy as np
from jax import lax
from jax.experimental import pallas as pl
from jax.experimental.pallas import tpu as pltpu
from jax.sharding import PartitionSpec as P

LAT = 16
ORBITAL_COUNT = 8
HALF = ORBITAL_COUNT * ORBITAL_COUNT
ROW = 2 * HALF
MEMORY_WEIGHT = 0.01
MIX_WEIGHT = 0.01
TIME_STEP = 0.1
HIGHEST = lax.Precision.HIGHEST
RUN = 4
VMEM_LIMIT = 20 * 1024 * 1024


def split(values):
    high = values.astype(jnp.bfloat16)
    return high, (values - high.astype(jnp.float32)).astype(jnp.bfloat16)


def lattice_tables():
    points, half = np.arange(LAT), np.arange(LAT // 2)
    kx, ky = np.repeat(half, LAT), np.tile(points, LAT // 2)
    tables = []
    for odd in range(2):
        rx, ry = np.repeat(2 * half + odd, LAT), np.tile(points, LAT // 2)
        angle = (rx[:, None] * kx[None, :] + ry[:, None] * ky[None, :]) % LAT * (2.0 * math.pi / LAT)
        tables.append([np.concatenate([np.cos(a), np.sin(a)]) for a in (angle, angle.T)])
    out = []
    for table in (np.stack([t[0] for t in tables]), np.stack([t[1] for t in tables])):
        table = table.astype(np.float32)
        high = table.astype(jnp.bfloat16)
        out += [np.concatenate([high, high], axis=2), (table - high.astype(np.float32)).astype(jnp.bfloat16)]
    return out


def dot(first, second):
    return lax.dot_general(first, second, (((1,), (0,)), ((), ())), preferred_element_type=jnp.float32)


def times_i(values, low):
    turned = pltpu.roll(values, HALF, 1)
    return jnp.where(low, -turned, turned)


def sigma_kernel(to_space_ref, to_space_low_ref, back_ref, back_low_ref, green_ref, screen_ref, out_ref):
    points = LAT * LAT
    half = points // 2
    slots = screen_ref.shape[0]
    first = lax.broadcasted_iota(jnp.int32, (half, ROW), 1) < HALF

    def turn(values, table, table_low, sign):
        high, low = split(values)
        both = dot(table, jnp.concatenate([high, low], axis=0)) + dot(table_low, high)
        out = []
        for i in range(2):
            here = both[:, i * ROW : (i + 1) * ROW]
            out.append(here[:half] + sign * times_i(here[half:], first))
        return out

    done = []
    for s in range(0, slots, 2):
        lower = jnp.concatenate([green_ref[: LAT // 2, s + i].reshape(half, ROW) for i in range(2)], axis=1)
        upper = jnp.concatenate([green_ref[LAT // 2 :, s + i].reshape(half, ROW) for i in range(2)], axis=1)
        turned = []
        for odd in range(2):
            space = turn(lower - upper if odd else lower + upper, to_space_ref[odd], to_space_low_ref[odd], 1.0)
            product = []
            for i in range(2):
                w = screen_ref[s + i].reshape(LAT // 2, 2, LAT, ROW)[:, odd].reshape(half, ROW) * (1.0 / points)
                w_turned = pltpu.roll(w, HALF, 1)
                g = space[i]
                g_turned = pltpu.roll(g, HALF, 1)
                product.append(g_turned * jnp.where(first, -w, w_turned) - g * jnp.where(first, w_turned, w))
            turned.append(turn(jnp.concatenate(product, axis=1), back_ref[odd], back_low_ref[odd], -1.0))
        for i in range(2):
            even, odd = turned[0][i], turned[1][i]
            done.append(jnp.concatenate([even + odd, even - odd], axis=0))
        if len(done) == 8:
            block = jnp.swapaxes(jnp.stack(done), 0, 1)
            out_ref[:, :, s - 6 : s + 2, :] = block.reshape(LAT, LAT, 8, ROW)
            done = []


def sigma_of(green, screen):
    slots = screen.shape[0]
    points = LAT * LAT
    return pl.pallas_call(
        sigma_kernel,
        out_shape=jax.ShapeDtypeStruct((LAT, LAT, slots, ROW), jnp.float32),
        compiler_params=pltpu.CompilerParams(vmem_limit_bytes=VMEM_LIMIT),
        cost_estimate=pl.CostEstimate(flops=slots * 8 * points * points * ROW, bytes_accessed=3 * slots * points * ROW * 4, transcendentals=0),
        name="sigma",
    )(*map(jnp.asarray, lattice_tables()), green, screen)


def history_kernel(high_ref, low_ref, sigma_ref, spread_ref, mixed_ref, out_ref):
    owners, _, slots, _ = sigma_ref.shape
    lane = lax.broadcasted_iota(jnp.int32, (ORBITAL_COUNT, ROW), 1)
    sub = lax.broadcasted_iota(jnp.int32, (ORBITAL_COUNT, ROW), 0)
    inner = lane % ORBITAL_COUNT
    blocks = []
    for k in range(LAT):
        rows = sigma_ref[:, k].reshape(owners * slots, ROW)
        s_high, s_low = split(rows)
        c_high, c_low = high_ref[k], low_ref[k]
        outer = dot(c_high, s_high) + (dot(c_high, s_low) + dot(c_low, s_high))
        outer = outer.reshape(2, ORBITAL_COUNT, ORBITAL_COUNT, ROW)
        for part in range(2):
            picked = jnp.zeros((ORBITAL_COUNT, ROW), jnp.float32)
            for b in range(ORBITAL_COUNT):
                picked = jnp.where(inner == b, outer[part, b], picked)
            blocks.append(picked)
    picked = jnp.concatenate(blocks, axis=0)
    p_high, p_rest = split(picked)
    p_low = p_rest
    spread = spread_ref[...]
    summed = dot(p_high, spread) + dot(p_low, spread)
    summed = summed.reshape(2 * LAT, ORBITAL_COUNT, ROW)
    summed = jnp.sum(jnp.where((inner == sub)[None], summed, 0.0), axis=1).reshape(LAT, 2, ROW)
    low_half = lax.broadcasted_iota(jnp.int32, (LAT, ROW), 1) < HALF
    total = MEMORY_WEIGHT * (summed[:, 0] + times_i(summed[:, 1], low_half)) + mixed_ref[...]
    out_ref[...] = jnp.broadcast_to(total[None], out_ref.shape)


def spread_table():
    group = np.arange(ROW) // ORBITAL_COUNT
    return (group[:, None] == group[None, :]).astype(jnp.bfloat16)


def history_of(high, low, sigma, mixed, copies):
    return pl.pallas_call(
        history_kernel,
        out_shape=jax.ShapeDtypeStruct((copies, LAT, ROW), jnp.float32),
        compiler_params=pltpu.CompilerParams(vmem_limit_bytes=VMEM_LIMIT),
        cost_estimate=pl.CostEstimate(flops=16 * 6 * 384 * ROW * ROW, bytes_accessed=2 * 384 * 16 * ROW * 4, transcendentals=0),
        name="history",
    )(high, low, sigma, jnp.asarray(spread_table()), mixed)


def complex_product(left, right):
    def contract(first, second):
        return jnp.einsum("kab,kbc->kac", first, second, precision=HIGHEST)

    return (
        contract(left[:, 0], right[:, 0]) - contract(left[:, 1], right[:, 1]),
        contract(left[:, 0], right[:, 1]) + contract(left[:, 1], right[:, 0]),
    )


def free_step(green_now, hamilton):
    shape = (green_now.shape[0], 2, ORBITAL_COUNT, ORBITAL_COUNT)
    green, ham = green_now.reshape(shape), hamilton.reshape(shape)
    left_re, left_im = complex_product(ham, green)
    right_re, right_im = complex_product(green, ham)
    moved = jnp.stack([left_im - right_im, right_re - left_re], axis=1)
    return green_now + TIME_STEP * moved.reshape(green_now.shape)


def mixed_sum(sigma_mix, green_mix):
    taus, points, _ = sigma_mix.shape
    left = sigma_mix.reshape(taus, points, 2, ORBITAL_COUNT, ORBITAL_COUNT)
    right = green_mix.reshape(taus, points, 2, ORBITAL_COUNT, ORBITAL_COUNT)

    def contract(first, second):
        return jnp.einsum("skab,skbc->kac", first, second, precision=HIGHEST).reshape(points, HALF)

    real = contract(left[:, :, 0], right[:, :, 0]) - contract(left[:, :, 1], right[:, :, 1])
    imag = contract(left[:, :, 0], right[:, :, 1]) + contract(left[:, :, 1], right[:, :, 0])
    return MIX_WEIGHT * jnp.concatenate([imag, -real], axis=-1)


def finish_kernel(parts_ref, free_ref, adjoint_ref, collision_ref, next_ref):
    collision = parts_ref[0]
    for i in range(1, parts_ref.shape[0]):
        collision = collision + parts_ref[i]
    high, rest = split(collision)
    middle, low = split(collision - high.astype(jnp.float32))
    adjoint = adjoint_ref[...]
    turned = dot(high, adjoint) + (dot(middle, adjoint) + dot(low, adjoint))
    collision_ref[...] = collision
    next_ref[...] = free_ref[...] - TIME_STEP * (collision + turned)


def adjoint_table():
    table = np.zeros((ROW, ROW), np.float32)
    for a in range(ORBITAL_COUNT):
        for c in range(ORBITAL_COUNT):
            table[a * ORBITAL_COUNT + c, c * ORBITAL_COUNT + a] = 1.0
            table[HALF + a * ORBITAL_COUNT + c, HALF + c * ORBITAL_COUNT + a] = -1.0
    return table.astype(jnp.bfloat16)


def finish(parts, free):
    out = jax.ShapeDtypeStruct(free.shape, jnp.float32)
    return pl.pallas_call(finish_kernel, out_shape=(out, out), name="finish")(parts, free, jnp.asarray(adjoint_table()))


def per_device(green_row, green_col, screen, filled, sigma_mix, green_mix, green_now, hamilton):
    slot_count, local_k, _ = green_row.shape
    owners = lax.axis_size("mom")
    own = slot_count // owners
    run = lax.axis_index("hist") // RUN
    early = (run + 1) // 2 % 2 == 1

    def local_work():
        return mixed_sum(sigma_mix, green_mix), free_step(green_now, hamilton)

    def nothing():
        return jax.tree.map(lambda leaf: jnp.zeros(leaf.shape, leaf.dtype), jax.eval_shape(local_work))

    ready = lax.cond(early, nothing, local_work)
    green_row, ready = lax.optimization_barrier((green_row, ready))
    moved = lax.all_to_all(green_row.reshape(owners, own, local_k, ROW), "mom", 0, 0)
    sigma = sigma_of(moved, screen)
    arrived = lax.all_to_all(sigma, "mom", 0, 0)
    valid = jnp.arange(slot_count, dtype=jnp.int32) < filled[0]
    column = jnp.where(valid[:, None, None], green_col, 0.0)
    column = jnp.transpose(column, (1, 2, 0))
    high = lax.reduce_precision(column, 8, 7)
    high, low = high.astype(jnp.bfloat16), (column - high).astype(jnp.bfloat16)
    ready, _ = lax.optimization_barrier((ready, moved))
    mixed, free = lax.cond(early, local_work, lambda: ready)
    partial_sums = history_of(high, low, arrived, mixed, lax.axis_size("hist"))
    parts = lax.all_to_all(partial_sums, "hist", 0, 0)
    return finish(parts, free)


def solution(mesh):
    return jax.shard_map(
        per_device,
        mesh=mesh,
        in_specs=(
            P("hist", "mom", None),
            P("hist", "mom", None),
            P(("hist", "mom"), None, None),
            P("hist"),
            P("hist", "mom", None),
            P("hist", "mom", None),
            P("mom", None),
            P("mom", None),
        ),
        out_specs=(P("mom", None), P("mom", None)),
        check_vma=False,
    )
```

```python
import functools
import math

import jax
import jax.numpy as jnp
import numpy as np
from jax import lax
from jax.experimental import pallas as pl
from jax.experimental.pallas import tpu as pltpu
from jax.sharding import PartitionSpec as P

LAT = 16
ORBITAL_COUNT = 8
HALF = ORBITAL_COUNT * ORBITAL_COUNT
ROW = 2 * HALF
MEMORY_WEIGHT = 0.01
MIX_WEIGHT = 0.01
TIME_STEP = 0.1
HIGHEST = lax.Precision.HIGHEST
RUN = 4
VMEM_LIMIT = 20 * 1024 * 1024


def exchange_order():
    return np.arange(LAT).reshape(2, 4, 2).swapaxes(0, 1).reshape(LAT)


def ordered(blocks):
    rest = blocks.shape[1:]
    return blocks.reshape(2, 4, 2, *rest).swapaxes(0, 1).reshape(LAT, *rest)


def exchange(blocks):
    groups = [[int(member) for member in exchange_order()]]
    return lax.all_to_all(blocks, "mom", 0, 0, axis_index_groups=groups)


def split(values):
    high = values.astype(jnp.bfloat16)
    return high, (values - high.astype(jnp.float32)).astype(jnp.bfloat16)


def lattice_tables():
    points, half = np.arange(LAT), np.arange(LAT // 2)
    kx, ky = np.repeat(half, LAT), np.tile(points, LAT // 2)
    tables = []
    for odd in range(2):
        rx, ry = np.repeat(2 * half + odd, LAT), np.tile(points, LAT // 2)
        angle = (rx[:, None] * kx[None, :] + ry[:, None] * ky[None, :]) % LAT * (2.0 * math.pi / LAT)
        tables.append([np.concatenate([np.cos(a), np.sin(a)]) for a in (angle, angle.T)])
    out = []
    for table in (np.stack([t[0] for t in tables]), np.stack([t[1] for t in tables])):
        table = table.astype(np.float32)
        high = table.astype(jnp.bfloat16)
        out += [np.concatenate([high, high], axis=2), (table - high.astype(np.float32)).astype(jnp.bfloat16)]
    return out


def dot(first, second):
    return lax.dot_general(first, second, (((1,), (0,)), ((), ())), preferred_element_type=jnp.float32)


def times_i(values, low):
    turned = pltpu.roll(values, HALF, 1)
    return jnp.where(low, -turned, turned)


def sigma_kernel(to_space_ref, to_space_low_ref, back_ref, back_low_ref, green_ref, screen_ref, out_ref):
    points = LAT * LAT
    half = points // 2
    slots = screen_ref.shape[0]
    first = lax.broadcasted_iota(jnp.int32, (half, ROW), 1) < HALF

    def turn(values, table, table_low, sign):
        high, low = split(values)
        both = dot(table, jnp.concatenate([high, low], axis=0)) + dot(table_low, high)
        out = []
        for i in range(2):
            here = both[:, i * ROW : (i + 1) * ROW]
            out.append(here[:half] + sign * times_i(here[half:], first))
        return out

    spots = [int(spot) for spot in np.argsort(exchange_order())]
    done = []
    for s in range(0, slots, 2):
        lower = jnp.concatenate([green_ref[: LAT // 2, s + i].reshape(half, ROW) for i in range(2)], axis=1)
        upper = jnp.concatenate([green_ref[LAT // 2 :, s + i].reshape(half, ROW) for i in range(2)], axis=1)
        turned = []
        for odd in range(2):
            space = turn(lower - upper if odd else lower + upper, to_space_ref[odd], to_space_low_ref[odd], 1.0)
            product = []
            for i in range(2):
                w = screen_ref[s + i].reshape(LAT // 2, 2, LAT, ROW)[:, odd].reshape(half, ROW) * (1.0 / points)
                w_turned = pltpu.roll(w, HALF, 1)
                g = space[i]
                g_turned = pltpu.roll(g, HALF, 1)
                product.append(g_turned * jnp.where(first, -w, w_turned) - g * jnp.where(first, w_turned, w))
            turned.append(turn(jnp.concatenate(product, axis=1), back_ref[odd], back_low_ref[odd], -1.0))
        for i in range(2):
            even, odd = turned[0][i], turned[1][i]
            done.append(jnp.concatenate([even + odd, even - odd], axis=0))
        if len(done) == 8:
            block = jnp.swapaxes(jnp.stack(done), 0, 1)
            block = block.reshape(LAT, LAT, 8, ROW)
            for kx in range(LAT):
                out_ref[spots[kx], :, s - 6 : s + 2, :] = block[kx]
            done = []


def sigma_of(green, screen):
    slots = screen.shape[0]
    points = LAT * LAT
    return pl.pallas_call(
        sigma_kernel,
        out_shape=jax.ShapeDtypeStruct((LAT, LAT, slots, ROW), jnp.float32),
        compiler_params=pltpu.CompilerParams(vmem_limit_bytes=VMEM_LIMIT),
        cost_estimate=pl.CostEstimate(flops=slots * 8 * points * points * ROW, bytes_accessed=3 * slots * points * ROW * 4, transcendentals=0),
        name="sigma",
    )(*map(jnp.asarray, lattice_tables()), green, screen)


def history_kernel(high_ref, low_ref, sigma_ref, spread_ref, mixed_ref, out_ref):
    owners, _, slots, _ = sigma_ref.shape
    lane = lax.broadcasted_iota(jnp.int32, (ORBITAL_COUNT, ROW), 1)
    sub = lax.broadcasted_iota(jnp.int32, (ORBITAL_COUNT, ROW), 0)
    inner = lane % ORBITAL_COUNT
    blocks = []
    for k in range(LAT):
        rows = sigma_ref[:, k].reshape(owners * slots, ROW)
        s_high, s_low = split(rows)
        c_high, c_low = high_ref[k], low_ref[k]
        outer = dot(c_high, s_high) + (dot(c_high, s_low) + dot(c_low, s_high))
        outer = outer.reshape(2, ORBITAL_COUNT, ORBITAL_COUNT, ROW)
        for part in range(2):
            picked = jnp.zeros((ORBITAL_COUNT, ROW), jnp.float32)
            for b in range(ORBITAL_COUNT):
                picked = jnp.where(inner == b, outer[part, b], picked)
            blocks.append(picked)
    picked = jnp.concatenate(blocks, axis=0)
    p_high, p_rest = split(picked)
    p_low = p_rest
    spread = spread_ref[...]
    summed = dot(p_high, spread) + dot(p_low, spread)
    summed = summed.reshape(2 * LAT, ORBITAL_COUNT, ROW)
    summed = jnp.sum(jnp.where((inner == sub)[None], summed, 0.0), axis=1).reshape(LAT, 2, ROW)
    low_half = lax.broadcasted_iota(jnp.int32, (LAT, ROW), 1) < HALF
    total = MEMORY_WEIGHT * (summed[:, 0] + times_i(summed[:, 1], low_half)) + mixed_ref[...]
    out_ref[...] = jnp.broadcast_to(total[None], out_ref.shape)


def spread_table():
    group = np.arange(ROW) // ORBITAL_COUNT
    return (group[:, None] == group[None, :]).astype(jnp.bfloat16)


def history_of(high, low, sigma, mixed, copies):
    return pl.pallas_call(
        history_kernel,
        out_shape=jax.ShapeDtypeStruct((copies, LAT, ROW), jnp.float32),
        compiler_params=pltpu.CompilerParams(vmem_limit_bytes=VMEM_LIMIT),
        cost_estimate=pl.CostEstimate(flops=16 * 6 * 384 * ROW * ROW, bytes_accessed=2 * 384 * 16 * ROW * 4, transcendentals=0),
        name="history",
    )(high, low, sigma, jnp.asarray(spread_table()), mixed)


def complex_product(left, right):
    def contract(first, second):
        return jnp.einsum("kab,kbc->kac", first, second, precision=HIGHEST)

    return (
        contract(left[:, 0], right[:, 0]) - contract(left[:, 1], right[:, 1]),
        contract(left[:, 0], right[:, 1]) + contract(left[:, 1], right[:, 0]),
    )


def free_step(green_now, hamilton):
    shape = (green_now.shape[0], 2, ORBITAL_COUNT, ORBITAL_COUNT)
    green, ham = green_now.reshape(shape), hamilton.reshape(shape)
    left_re, left_im = complex_product(ham, green)
    right_re, right_im = complex_product(green, ham)
    moved = jnp.stack([left_im - right_im, right_re - left_re], axis=1)
    return green_now + TIME_STEP * moved.reshape(green_now.shape)


def mixed_sum(sigma_mix, green_mix):
    taus, points, _ = sigma_mix.shape
    left = sigma_mix.reshape(taus, points, 2, ORBITAL_COUNT, ORBITAL_COUNT)
    right = green_mix.reshape(taus, points, 2, ORBITAL_COUNT, ORBITAL_COUNT)

    def contract(first, second):
        return jnp.einsum("skab,skbc->kac", first, second, precision=HIGHEST).reshape(points, HALF)

    real = contract(left[:, :, 0], right[:, :, 0]) - contract(left[:, :, 1], right[:, :, 1])
    imag = contract(left[:, :, 0], right[:, :, 1]) + contract(left[:, :, 1], right[:, :, 0])
    return MIX_WEIGHT * jnp.concatenate([imag, -real], axis=-1)


def finish_kernel(parts_ref, free_ref, adjoint_ref, collision_ref, next_ref):
    collision = parts_ref[0]
    for i in range(1, parts_ref.shape[0]):
        collision = collision + parts_ref[i]
    high, rest = split(collision)
    middle, low = split(collision - high.astype(jnp.float32))
    adjoint = adjoint_ref[...]
    turned = dot(high, adjoint) + (dot(middle, adjoint) + dot(low, adjoint))
    collision_ref[...] = collision
    next_ref[...] = free_ref[...] - TIME_STEP * (collision + turned)


def adjoint_table():
    table = np.zeros((ROW, ROW), np.float32)
    for a in range(ORBITAL_COUNT):
        for c in range(ORBITAL_COUNT):
            table[a * ORBITAL_COUNT + c, c * ORBITAL_COUNT + a] = 1.0
            table[HALF + a * ORBITAL_COUNT + c, HALF + c * ORBITAL_COUNT + a] = -1.0
    return table.astype(jnp.bfloat16)


def finish(parts, free):
    out = jax.ShapeDtypeStruct(free.shape, jnp.float32)
    return pl.pallas_call(finish_kernel, out_shape=(out, out), name="finish")(parts, free, jnp.asarray(adjoint_table()))


def per_device(green_row, green_col, screen, filled, sigma_mix, green_mix, green_now, hamilton):
    slot_count, local_k, _ = green_row.shape
    owners = lax.axis_size("mom")
    own = slot_count // owners
    run = lax.axis_index("hist") // RUN
    early = (run + 1) // 2 % 2 == 1

    def local_work():
        return mixed_sum(sigma_mix, green_mix), free_step(green_now, hamilton)

    def nothing():
        return jax.tree.map(lambda leaf: jnp.zeros(leaf.shape, leaf.dtype), jax.eval_shape(local_work))

    ready = lax.cond(early, nothing, local_work)
    green_row, ready = lax.optimization_barrier((green_row, ready))
    moved = lax.all_to_all(green_row.reshape(owners, own, local_k, ROW), "mom", 0, 0)
    sigma = sigma_of(moved, screen)
    arrived = exchange(sigma)
    valid = jnp.arange(slot_count, dtype=jnp.int32) < filled[0]
    column = jnp.where(valid[:, None, None], green_col, 0.0)
    column = ordered(column.reshape(owners, own, local_k, ROW)).reshape(slot_count, local_k, ROW)
    column = jnp.transpose(column, (1, 2, 0))
    high = lax.reduce_precision(column, 8, 7)
    high, low = high.astype(jnp.bfloat16), (column - high).astype(jnp.bfloat16)
    ready, _ = lax.optimization_barrier((ready, moved))
    mixed, free = lax.cond(early, local_work, lambda: ready)
    partial_sums = history_of(high, low, arrived, mixed, lax.axis_size("hist"))
    parts = lax.all_to_all(partial_sums, "hist", 0, 0)
    return finish(parts, free)


def solution(mesh):
    return jax.shard_map(
        per_device,
        mesh=mesh,
        in_specs=(
            P("hist", "mom", None),
            P("hist", "mom", None),
            P(("hist", "mom"), None, None),
            P("hist"),
            P("hist", "mom", None),
            P("hist", "mom", None),
            P("mom", None),
            P("mom", None),
        ),
        out_specs=(P("mom", None), P("mom", None)),
        check_vma=False,
    )
```

```python
import functools
import math

import jax
import jax.numpy as jnp
import numpy as np
from jax import lax
from jax.experimental import pallas as pl
from jax.experimental.pallas import tpu as pltpu
from jax.sharding import PartitionSpec as P

LAT = 16
ORBITAL_COUNT = 8
HALF = ORBITAL_COUNT * ORBITAL_COUNT
ROW = 2 * HALF
MEMORY_WEIGHT = 0.01
MIX_WEIGHT = 0.01
TIME_STEP = 0.1
HIGHEST = lax.Precision.HIGHEST
RUN = 4
VMEM_LIMIT = 20 * 1024 * 1024


def exchange_order():
    return np.arange(LAT).reshape(2, 8).swapaxes(0, 1).reshape(LAT)


def ordered(blocks):
    rest = blocks.shape[1:]
    return blocks.reshape(2, 8, *rest).swapaxes(0, 1).reshape(LAT, *rest)


def exchange(blocks):
    groups = [[int(member) for member in exchange_order()]]
    return lax.all_to_all(blocks, "mom", 0, 0, axis_index_groups=groups)


def split(values):
    high = values.astype(jnp.bfloat16)
    return high, (values - high.astype(jnp.float32)).astype(jnp.bfloat16)


def lattice_tables():
    points, half = np.arange(LAT), np.arange(LAT // 2)
    kx, ky = np.repeat(half, LAT), np.tile(points, LAT // 2)
    tables = []
    for odd in range(2):
        rx, ry = np.repeat(2 * half + odd, LAT), np.tile(points, LAT // 2)
        angle = (rx[:, None] * kx[None, :] + ry[:, None] * ky[None, :]) % LAT * (2.0 * math.pi / LAT)
        tables.append([np.concatenate([np.cos(a), np.sin(a)]) for a in (angle, angle.T)])
    out = []
    for table in (np.stack([t[0] for t in tables]), np.stack([t[1] for t in tables])):
        table = table.astype(np.float32)
        high = table.astype(jnp.bfloat16)
        out += [np.concatenate([high, high], axis=2), (table - high.astype(np.float32)).astype(jnp.bfloat16)]
    return out


def dot(first, second):
    return lax.dot_general(first, second, (((1,), (0,)), ((), ())), preferred_element_type=jnp.float32)


def times_i(values, low):
    turned = pltpu.roll(values, HALF, 1)
    return jnp.where(low, -turned, turned)


def sigma_kernel(to_space_ref, to_space_low_ref, back_ref, back_low_ref, green_ref, screen_ref, out_ref):
    points = LAT * LAT
    half = points // 2
    slots = screen_ref.shape[0]
    first = lax.broadcasted_iota(jnp.int32, (half, ROW), 1) < HALF

    def turn(values, table, table_low, sign):
        high, low = split(values)
        both = dot(table, jnp.concatenate([high, low], axis=0)) + dot(table_low, high)
        out = []
        for i in range(2):
            here = both[:, i * ROW : (i + 1) * ROW]
            out.append(here[:half] + sign * times_i(here[half:], first))
        return out

    spots = [int(spot) for spot in np.argsort(exchange_order())]
    done = []
    for s in range(0, slots, 2):
        lower = jnp.concatenate([green_ref[: LAT // 2, s + i].reshape(half, ROW) for i in range(2)], axis=1)
        upper = jnp.concatenate([green_ref[LAT // 2 :, s + i].reshape(half, ROW) for i in range(2)], axis=1)
        turned = []
        for odd in range(2):
            space = turn(lower - upper if odd else lower + upper, to_space_ref[odd], to_space_low_ref[odd], 1.0)
            product = []
            for i in range(2):
                w = screen_ref[s + i].reshape(LAT // 2, 2, LAT, ROW)[:, odd].reshape(half, ROW) * (1.0 / points)
                w_turned = pltpu.roll(w, HALF, 1)
                g = space[i]
                g_turned = pltpu.roll(g, HALF, 1)
                product.append(g_turned * jnp.where(first, -w, w_turned) - g * jnp.where(first, w_turned, w))
            turned.append(turn(jnp.concatenate(product, axis=1), back_ref[odd], back_low_ref[odd], -1.0))
        for i in range(2):
            even, odd = turned[0][i], turned[1][i]
            done.append(jnp.concatenate([even + odd, even - odd], axis=0))
        if len(done) == 8:
            block = jnp.swapaxes(jnp.stack(done), 0, 1)
            block = block.reshape(LAT, LAT, 8, ROW)
            for kx in range(LAT):
                out_ref[spots[kx], :, s - 6 : s + 2, :] = block[kx]
            done = []


def sigma_of(green, screen):
    slots = screen.shape[0]
    points = LAT * LAT
    return pl.pallas_call(
        sigma_kernel,
        out_shape=jax.ShapeDtypeStruct((LAT, LAT, slots, ROW), jnp.float32),
        compiler_params=pltpu.CompilerParams(vmem_limit_bytes=VMEM_LIMIT),
        cost_estimate=pl.CostEstimate(flops=slots * 8 * points * points * ROW, bytes_accessed=3 * slots * points * ROW * 4, transcendentals=0),
        name="sigma",
    )(*map(jnp.asarray, lattice_tables()), green, screen)


def history_kernel(high_ref, low_ref, sigma_ref, spread_ref, mixed_ref, out_ref):
    owners, _, slots, _ = sigma_ref.shape
    lane = lax.broadcasted_iota(jnp.int32, (ORBITAL_COUNT, ROW), 1)
    sub = lax.broadcasted_iota(jnp.int32, (ORBITAL_COUNT, ROW), 0)
    inner = lane % ORBITAL_COUNT
    blocks = []
    for k in range(LAT):
        rows = sigma_ref[:, k].reshape(owners * slots, ROW)
        s_high, s_low = split(rows)
        c_high, c_low = high_ref[k], low_ref[k]
        outer = dot(c_high, s_high) + (dot(c_high, s_low) + dot(c_low, s_high))
        outer = outer.reshape(2, ORBITAL_COUNT, ORBITAL_COUNT, ROW)
        for part in range(2):
            picked = jnp.zeros((ORBITAL_COUNT, ROW), jnp.float32)
            for b in range(ORBITAL_COUNT):
                picked = jnp.where(inner == b, outer[part, b], picked)
            blocks.append(picked)
    picked = jnp.concatenate(blocks, axis=0)
    p_high, p_rest = split(picked)
    p_low = p_rest
    spread = spread_ref[...]
    summed = dot(p_high, spread) + dot(p_low, spread)
    summed = summed.reshape(2 * LAT, ORBITAL_COUNT, ROW)
    summed = jnp.sum(jnp.where((inner == sub)[None], summed, 0.0), axis=1).reshape(LAT, 2, ROW)
    low_half = lax.broadcasted_iota(jnp.int32, (LAT, ROW), 1) < HALF
    total = MEMORY_WEIGHT * (summed[:, 0] + times_i(summed[:, 1], low_half)) + mixed_ref[...]
    out_ref[...] = jnp.broadcast_to(total[None], out_ref.shape)


def spread_table():
    group = np.arange(ROW) // ORBITAL_COUNT
    return (group[:, None] == group[None, :]).astype(jnp.bfloat16)


def history_of(high, low, sigma, mixed, copies):
    return pl.pallas_call(
        history_kernel,
        out_shape=jax.ShapeDtypeStruct((copies, LAT, ROW), jnp.float32),
        compiler_params=pltpu.CompilerParams(vmem_limit_bytes=VMEM_LIMIT),
        cost_estimate=pl.CostEstimate(flops=16 * 6 * 384 * ROW * ROW, bytes_accessed=2 * 384 * 16 * ROW * 4, transcendentals=0),
        name="history",
    )(high, low, sigma, jnp.asarray(spread_table()), mixed)


def complex_product(left, right):
    def contract(first, second):
        return jnp.einsum("kab,kbc->kac", first, second, precision=HIGHEST)

    return (
        contract(left[:, 0], right[:, 0]) - contract(left[:, 1], right[:, 1]),
        contract(left[:, 0], right[:, 1]) + contract(left[:, 1], right[:, 0]),
    )


def free_step(green_now, hamilton):
    shape = (green_now.shape[0], 2, ORBITAL_COUNT, ORBITAL_COUNT)
    green, ham = green_now.reshape(shape), hamilton.reshape(shape)
    left_re, left_im = complex_product(ham, green)
    right_re, right_im = complex_product(green, ham)
    moved = jnp.stack([left_im - right_im, right_re - left_re], axis=1)
    return green_now + TIME_STEP * moved.reshape(green_now.shape)


def mixed_sum(sigma_mix, green_mix):
    taus, points, _ = sigma_mix.shape
    left = sigma_mix.reshape(taus, points, 2, ORBITAL_COUNT, ORBITAL_COUNT)
    right = green_mix.reshape(taus, points, 2, ORBITAL_COUNT, ORBITAL_COUNT)

    def contract(first, second):
        return jnp.einsum("skab,skbc->kac", first, second, precision=HIGHEST).reshape(points, HALF)

    real = contract(left[:, :, 0], right[:, :, 0]) - contract(left[:, :, 1], right[:, :, 1])
    imag = contract(left[:, :, 0], right[:, :, 1]) + contract(left[:, :, 1], right[:, :, 0])
    return MIX_WEIGHT * jnp.concatenate([imag, -real], axis=-1)


def finish_kernel(parts_ref, free_ref, adjoint_ref, collision_ref, next_ref):
    collision = parts_ref[0]
    for i in range(1, parts_ref.shape[0]):
        collision = collision + parts_ref[i]
    high, rest = split(collision)
    middle, low = split(collision - high.astype(jnp.float32))
    adjoint = adjoint_ref[...]
    turned = dot(high, adjoint) + (dot(middle, adjoint) + dot(low, adjoint))
    collision_ref[...] = collision
    next_ref[...] = free_ref[...] - TIME_STEP * (collision + turned)


def adjoint_table():
    table = np.zeros((ROW, ROW), np.float32)
    for a in range(ORBITAL_COUNT):
        for c in range(ORBITAL_COUNT):
            table[a * ORBITAL_COUNT + c, c * ORBITAL_COUNT + a] = 1.0
            table[HALF + a * ORBITAL_COUNT + c, HALF + c * ORBITAL_COUNT + a] = -1.0
    return table.astype(jnp.bfloat16)


def finish(parts, free):
    out = jax.ShapeDtypeStruct(free.shape, jnp.float32)
    return pl.pallas_call(finish_kernel, out_shape=(out, out), name="finish")(parts, free, jnp.asarray(adjoint_table()))


def per_device(green_row, green_col, screen, filled, sigma_mix, green_mix, green_now, hamilton):
    slot_count, local_k, _ = green_row.shape
    owners = lax.axis_size("mom")
    own = slot_count // owners
    run = lax.axis_index("hist") // RUN
    early = (run + 1) // 2 % 2 == 1

    def local_work():
        return mixed_sum(sigma_mix, green_mix), free_step(green_now, hamilton)

    def nothing():
        return jax.tree.map(lambda leaf: jnp.zeros(leaf.shape, leaf.dtype), jax.eval_shape(local_work))

    ready = lax.cond(early, nothing, local_work)
    green_row, ready = lax.optimization_barrier((green_row, ready))
    moved = lax.all_to_all(green_row.reshape(owners, own, local_k, ROW), "mom", 0, 0)
    sigma = sigma_of(moved, screen)
    arrived = exchange(sigma)
    valid = jnp.arange(slot_count, dtype=jnp.int32) < filled[0]
    column = jnp.where(valid[:, None, None], green_col, 0.0)
    column = ordered(column.reshape(owners, own, local_k, ROW)).reshape(slot_count, local_k, ROW)
    column = jnp.transpose(column, (1, 2, 0))
    high = lax.reduce_precision(column, 8, 7)
    high, low = high.astype(jnp.bfloat16), (column - high).astype(jnp.bfloat16)
    ready, _ = lax.optimization_barrier((ready, moved))
    mixed, free = lax.cond(early, local_work, lambda: ready)
    partial_sums = history_of(high, low, arrived, mixed, lax.axis_size("hist"))
    parts = lax.all_to_all(partial_sums, "hist", 0, 0)
    return finish(parts, free)


def solution(mesh):
    return jax.shard_map(
        per_device,
        mesh=mesh,
        in_specs=(
            P("hist", "mom", None),
            P("hist", "mom", None),
            P(("hist", "mom"), None, None),
            P("hist"),
            P("hist", "mom", None),
            P("hist", "mom", None),
            P("mom", None),
            P("mom", None),
        ),
        out_specs=(P("mom", None), P("mom", None)),
        check_vma=False,
    )
```
